32 devices in a mesh: grp: 2 (over y), doc: 4 (over x, core), voc: 4 (over z).
Axes of the slice: x: 2, y: 2, z: 4, core: 2. Of those that a mesh axis runs over, the one named last changes fastest.
Arguments:
- hidden: bfloat16 [48, 256, 768], P(('grp', 'doc')), parts along dimension 0, may hold values from -6 to 6
- lengths: int32 [48], P(('grp', 'doc')), parts along dimension 0, may hold values from 1 to 256, 3840 in all
- w_trans: bfloat16 [768, 768], replicated, may hold values from -0.21875 to 0.21875
- b_trans: float32 [768], replicated, may hold values from -3 to 3
- ln_gain: float32 [768], replicated, may hold values from 0.5 to 1.5
- ln_bias: float32 [768], replicated, may hold values from -3 to 3
- w_decode: bfloat16 [768, 30720], P(None, 'voc'), may hold values from -0.21875 to 0.21875
- b_decode: float32 [30720], P('voc'), may hold values from -5 to 5
- query_ids: int32 [2048, 32], P('grp'), parts along dimension 0, may hold values from 0 to 30719
- query_wts: int32 [2048, 32], P('grp'), parts along dimension 0, may hold values from 1 to 100
Outputs:
- scores: float32 [48, 1024], P(('grp', 'voc'), 'doc'), parts along dimension 0
The draws below stay inside these ranges and needn't reach their ends.
There are 2 independent parts, one for each index of `grp`. The reference program is written for one: setup_inputs(seed, part) draws one part's arguments, and reference() takes and returns one part's arrays. A program takes and returns all parts, laid end to end along the dimension named above; an argument that names none is the same for every part. Nothing has to cross between parts.
Inputs may be any that keep to these rules, and one draw needn't show every extreme that they name: Every passage has at least one live token and the longest has exactly 256. Within each grp group the 24 lengths sum to 3840; over the whole array, which holds both groups, the sum is twice that.
All inputs are finite; a program needn't handle non-finite values.
Results may differ from the reference program's by a relative error of at most 0.0003.
Values sent between devices are 32-bit elements; how exact they have to be, the bound alone decides.
No kernel may reach another device: no remote copies, remote signals or barrier semaphores. Data moves between devices by JAX's collectives and lax.ppermute only.
A program may use at most 64 MiB of HBM per device.

```python
import math
import jax
import jax.numpy as jnp
import numpy as np
from jax import lax

D = 768
V = 30720
L = 256
QT = 32
P_SIZE = 24
Q = 1024


def plant(result, stream_key, smallest, largest):
    index_at = [jax.random.randint(jax.random.fold_in(stream_key, axis), (), 0, length) for axis, length in enumerate(result.shape)]
    main_axis = result.shape.index(max(result.shape))
    next_to = index_at[:main_axis] + [(index_at[main_axis] + 1) % result.shape[main_axis]] + index_at[main_axis + 1:]
    return result.at[tuple(index_at)].set(smallest).at[tuple(next_to)].set(largest)


def levels(stream_key, dims, cuts, least, top_value):
    gain, own = 1.0, jax.random.fold_in(stream_key, 6)
    for position, parts in cuts:
        steps = jnp.exp(jax.random.uniform(jax.random.fold_in(own, position), (parts,), jnp.float32, least / len(cuts), top_value / len(cuts)))
        gain = gain * jnp.repeat(steps, dims[position] // parts).reshape([-1 if axis == position else 1 for axis in range(len(dims))])
    return gain


def length_profile(number_of, total, limit, lean):
    loads = [(1 << 20) // math.isqrt(standing ** lean) + 1 for standing in range(2, number_of + 1)]
    spare, counts = total - limit - (number_of - 1), [1] * (number_of - 1)
    while spare > 0:
        free = [i for i in range(number_of - 1) if counts[i] < limit]
        pool, budget = sum([loads[i] for i in free]), spare
        for i in free:
            extra = min(limit - counts[i], max(1, budget * loads[i] // pool), spare)
            counts[i] = counts[i] + extra
            spare = spare - extra
    return np.array([limit] + counts)


def ragged(own_key, count, total, reach, lean):
    if count == 2:
        one = jax.random.randint(own_key, (), max(1, total - reach), min(reach, total - 1) + 1)
        return jnp.stack([one, total - one])
    sizes = jnp.asarray(length_profile(count, total, reach, lean), jnp.int32)
    twos = (count - 1) // 2
    source_of, sink = sizes[1:1 + 2 * twos:2], sizes[2:2 + 2 * twos:2]
    slack = jnp.minimum(source_of - 1, reach - sink)
    moved = jax.random.randint(jax.random.fold_in(own_key, 1), (twos,), 0, 1 << 20) % (slack + 1)
    sizes = sizes.at[1:1 + 2 * twos:2].set(source_of - moved).at[2:2 + 2 * twos:2].set(sink + moved)
    return sizes[jax.random.permutation(jax.random.fold_in(own_key, 2), count)]


def gaussian(stream_key, shape, scale, bound, shards=(), held_as=jnp.bfloat16):
    result = jax.random.normal(stream_key, shape, jnp.float32) * scale
    if len(shards) > 0:
        result = levels(stream_key, shape, shards, -0.22, 0.18) * result
    return jnp.clip(result, min=-bound, max=bound).astype(held_as)


def setup_inputs(seed: int = 0, part: int = 0) -> dict:
    splits = jax.random.split(jax.random.key(seed), 11)
    part_keys = jax.random.split(jax.random.fold_in(splits[10], part), 11)
    return {
        "hidden": gaussian(part_keys[0], (P_SIZE, L, D), 1.0, 6.0, ((0, 4),)),
        "lengths": ragged(part_keys[1], P_SIZE, P_SIZE * L * 5 // 8, L, 1).astype(jnp.int32),
        "w_trans": gaussian(splits[2], (D, D), D ** -0.5, 0.21875),
        "b_trans": gaussian(splits[3], (D,), 0.5, 3.0, (), jnp.float32),
        "ln_gain": jnp.clip(jax.random.uniform(splits[4], (D,), jnp.float32, 0.5, 1.5), 0.5, 1.5),
        "ln_bias": gaussian(splits[5], (D,), 0.5, 3.0, (), jnp.float32),
        "w_decode": gaussian(splits[6], (D, V), D ** -0.5, 0.21875, ((1, 4),)),
        "b_decode": gaussian(splits[7], (V,), 1.0, 5.0, ((0, 4),), jnp.float32),
        "query_ids": plant(jax.random.randint(part_keys[8], (Q, QT), 0, V), jax.random.fold_in(part_keys[8], 1), 0, V - 1).astype(jnp.int32),
        "query_wts": plant(jax.random.randint(part_keys[9], (Q, QT), 1, 101), jax.random.fold_in(part_keys[9], 1), 1, 100).astype(jnp.int32),
    }


eps = 1e-06
score_scale = 1.0 / 1024.0
dead_fill = -1e+30

def transform(hidden, w_trans, b_trans, ln_gain, ln_bias):
    count, length, width = hidden.shape
    flat = hidden.reshape(count * length, width)
    pre = jnp.dot(flat, w_trans, preferred_element_type=jnp.float32) + b_trans
    active = jax.nn.gelu(pre, approximate=False)
    centre = active - lax.optimization_barrier(jnp.mean(active, -1, keepdims=True))
    spread = lax.optimization_barrier(jnp.mean(centre * centre, -1, keepdims=True))
    normed = centre * lax.rsqrt(spread + eps) * ln_gain + ln_bias
    return normed.astype(jnp.bfloat16).reshape(count, length, width)

def reference(hidden, lengths, w_trans, b_trans, ln_gain, ln_bias, w_decode, b_decode, query_ids, query_wts):
    transformed = transform(hidden, w_trans, b_trans, ln_gain, ln_bias)
    decode_full = w_decode.astype(jnp.float32)

    def pool_rows(pair):
        passage, live = pair
        logits = jnp.dot(passage.astype(jnp.float32), decode_full) + b_decode
        inside = jnp.arange(passage.shape[0], dtype=jnp.int32)[:, None] < live
        top = lax.optimization_barrier(jnp.max(jnp.where(inside, logits, jnp.full_like(logits, dead_fill)), 0))
        return jnp.log1p(jnp.maximum(top, jnp.zeros_like(top)))
    impacts = lax.map(pool_rows, (transformed, lengths))
    weights = query_wts.astype(jnp.float32)
    picked = impacts[:, query_ids]
    return lax.optimization_barrier(jnp.sum(picked * weights[None], -1)) * score_scale
```

```python
import functools

import jax
import jax.numpy as jnp
from jax import lax
from jax.experimental import pallas as pl
from jax.experimental.pallas import tpu as pltpu
from jax.sharding import PartitionSpec as P

eps = 1e-06
score_scale = 1.0 / 1024.0
group_rows = 16
lo_terms = 256
half_root = 0.7071067811865476


def ceil_to(value, unit):
    return -(-value // unit) * unit


def largest_tile(width, unit, limit):
    best = unit
    for size in range(unit, min(width, limit) + 1, unit):
        if width % size == 0:
            best = size
    return best


def norm_rows(pre, bias, gain, shift):
    x = pre + bias
    active = 0.5 * x * (1.0 + lax.erf(x * half_root))
    width = active.shape[-1]
    centre = active - jnp.sum(active, -1, keepdims=True) * (1.0 / width)
    spread = jnp.sum(centre * centre, -1, keepdims=True) * (1.0 / width)
    return centre * lax.rsqrt(spread + eps) * gain + shift


def compact(ids_ref, wts_ref, start, width, slots_ref):
    local = ids_ref[...] - start
    inside = (local >= 0) & (local < width)
    count = local.shape[0]
    outside = jnp.where(inside, 0, 1)

    def up(x, s):
        return jnp.concatenate([x[s:], jnp.zeros_like(x[:s])], 0)

    def down(x, s):
        return jnp.concatenate([jnp.zeros_like(x[:s]), x[:-s]], 0)

    before = outside
    step = 1
    while step < count:
        before = before + down(before, step)
        step *= 2
    key = jnp.where(inside, (before << 23) | (local << 8) | wts_ref[...], 0)
    step, bit = 1, 23
    while step < count:
        moves = (key >> bit) & 1
        stay = jnp.where(moves == 0, key, 0)
        come = jnp.where(moves == 0, 0, key)
        key = stay | up(come, step)
        step *= 2
        bit += 1
    key = key & ((1 << 23) - 1)
    for k in range(count):
        slots_ref[k] = key[k : k + 1]
    lane_counts = count - before[count - 1 :]
    return lane_counts


def kernel(
    sizes,
    len_ref,
    hid_hbm,
    wt_hbm,
    bt_ref,
    gain_ref,
    shift_ref,
    wd_hbm,
    bd_ref,
    ids_ref,
    wts_ref,
    *rest,
):
    n_pass, length, width, terms, n_doc, n_voc, q_own, chunk, tile = sizes
    outs = rest[:n_doc]
    hid, wt, wd, tok, pre, acc, carry, tabf, tab, slots, offs, sem_h, sem_t, sem_w = rest[n_doc:]
    n_tile = terms // tile
    n_group = chunk // group_rows
    n_hi = tabf.shape[1]

    hid_copies = [pltpu.make_async_copy(hid_hbm.at[p], hid.at[p], sem_h.at[p]) for p in range(n_pass)]
    wt_copy = pltpu.make_async_copy(wt_hbm, wt, sem_t)
    wd_copies = [
        pltpu.make_async_copy(
            wd_hbm.at[:, pl.ds(t * tile, tile)], wd.at[:, pl.ds(t * tile, tile)], sem_w.at[t]
        )
        for t in range(n_tile)
    ]
    hid_copies[0].start()
    wt_copy.start()
    for copy in hid_copies[1:]:
        copy.start()
    for copy in wd_copies:
        copy.start()

    doc, voc = lax.axis_index("doc"), lax.axis_index("voc")
    lane_counts = compact(ids_ref, wts_ref, voc * terms, terms, slots)
    most = jnp.max(lane_counts)

    at = jnp.int32(0)
    starts = []
    for p in range(n_pass):
        starts.append(at)
        at = at + (len_ref[p] + (group_rows - 1)) // group_rows
    total = at
    starts.append(total)
    n_chunk = (total + (n_group - 1)) // n_group

    for p in range(n_pass):
        hid_copies[p].wait()
        base = pl.multiple_of(starts[p] * group_rows, group_rows)
        tok[pl.ds(base, length), :] = hid[p]
        last = (len_ref[p] - 1) // group_rows * group_rows
        rows = hid[p, pl.ds(pl.multiple_of(last, group_rows), group_rows), :].astype(jnp.float32)
        live = lax.broadcasted_iota(jnp.int32, rows.shape, 0) < len_ref[p] - last
        fixed = jnp.where(live, rows, rows[0:1])
        tok[pl.ds(pl.multiple_of(base + last, group_rows), group_rows), :] = fixed.astype(jnp.bfloat16)
    wt_copy.wait()

    def project(c):
        rows = pl.ds(pl.multiple_of(c * chunk, group_rows), chunk)
        pre[...] = jnp.dot(tok[rows, :], wt[...], preferred_element_type=jnp.float32)

    def normalise(c, g):
        normed = norm_rows(
            pre[g * group_rows : (g + 1) * group_rows, :], bt_ref[...], gain_ref[...], shift_ref[...]
        )
        rows = pl.ds(pl.multiple_of(c * chunk + g * group_rows, group_rows), group_rows)
        tok[rows, :] = normed.astype(jnp.bfloat16)

    project(0)
    for g in range(n_group):
        normalise(0, g)
    carry[...] = jnp.zeros_like(carry)
    for copy in wd_copies:
        copy.wait()

    def decode(c, ahead):
        segs, firsts = [], []
        for g in range(n_group):
            group = c * n_group + g
            seg = jnp.int32(0)
            first = group == 0
            for p in range(1, n_pass + 1):
                seg = seg + jnp.where(group >= starts[p], 1, 0)
                first = first | (group == starts[p])
            segs.append(seg)
            firsts.append(first)
        rows = pl.ds(pl.multiple_of(c * chunk, group_rows), chunk)
        if ahead:
            project(c + 1)
        for t in range(n_tile):
            cols = slice(t * tile, (t + 1) * tile)
            logits = jnp.dot(tok[rows, :], wd[:, cols], preferred_element_type=jnp.float32)
            run = carry[:, cols]
            for g in range(n_group):
                r = g * group_rows
                top = jnp.maximum(logits[r : r + 8], logits[r + 8 : r + 16])
                run = jnp.where(firsts[g], top, jnp.maximum(run, top))
                acc[segs[g], :, cols] = run
            carry[:, cols] = run
            if ahead:
                for g in range(n_group * t // n_tile, n_group * (t + 1) // n_tile):
                    normalise(c + 1, g)

    @pl.loop(0, n_chunk)
    def _(c):
        decode(c, True)

    tabf[...] = jnp.zeros_like(tabf)
    for p in range(n_pass):
        for h in range(-(-terms // lo_terms)):
            cols = slice(h * lo_terms, min((h + 1) * lo_terms, terms))
            tabf[p, h : h + 1, : cols.stop - cols.start] = (
                jnp.max(acc[p, :, cols], 0, keepdims=True) + bd_ref[:, cols]
            )
    for p in range(n_pass):
        impacts = jnp.log1p(jnp.maximum(tabf[p], 0.0))
        upper = impacts.astype(jnp.bfloat16)
        lower = (impacts - upper.astype(jnp.float32)).astype(jnp.bfloat16)
        tab[p * n_hi : (p + 1) * n_hi, :] = upper
        tab[(n_pass + p) * n_hi : (n_pass + p + 1) * n_hi, :] = lower

    sub = lax.broadcasted_iota(jnp.int32, (lo_terms, q_own), 0)
    hi_sub = lax.broadcasted_iota(jnp.int32, (n_hi, q_own), 0)
    ratio = max(n_doc // n_voc, 1)
    for r in range(n_doc):
        block = lax.rem(lax.rem(doc, ratio) * n_voc + voc + r, n_doc)
        lanes = pl.ds(pl.multiple_of(block * q_own, 128), q_own)

        def add_slot(k, sums):
            key = slots[k, :, lanes]
            weight = (key & 255).astype(jnp.float32)
            term = key >> 8
            hot = jnp.where(sub == (term & (lo_terms - 1)), 1.0, 0.0).astype(jnp.bfloat16)
            found = jnp.dot(tab[...], hot, preferred_element_type=jnp.float32)
            pick = jnp.where(hi_sub == term // lo_terms, weight, 0.0)
            out = []
            for p in range(n_pass):
                a = p * n_hi
                b = (n_pass + p) * n_hi
                value = (found[a : a + n_hi] + found[b : b + n_hi]) * pick
                out.append(sums[p] + jnp.sum(value.reshape(n_hi // 8, 8, q_own), 0))
            return tuple(out)

        sums = lax.fori_loop(
            0, most, add_slot, tuple(jnp.zeros((8, q_own), jnp.float32) for _ in range(n_pass))
        )
        for p in range(n_pass):
            outs[r][p : p + 1, :] = jnp.sum(sums[p], 0, keepdims=True) * score_scale


def shards(
    n_doc, n_voc, hidden, lengths, w_trans, b_trans, ln_gain, ln_bias, w_decode, b_decode, query_ids, query_wts
):
    n_pass, length, width = hidden.shape
    terms = w_decode.shape[1]
    n_query, n_slot = query_ids.shape
    q_own = n_query // n_doc
    chunk = 256
    tile = largest_tile(terms, 128, 512)
    n_hi = ceil_to(-(-terms // lo_terms), 8)
    rows = ceil_to(n_pass * length, chunk) + chunk
    sizes = (n_pass, length, width, terms, n_doc, n_voc, q_own, chunk, tile)
    vmem = pl.BlockSpec(memory_space=pltpu.VMEM)
    anywhere = pl.BlockSpec(memory_space=pl.ANY)
    blocks = pl.pallas_call(
        functools.partial(kernel, sizes),
        out_shape=[jax.ShapeDtypeStruct((n_pass, q_own), jnp.float32)] * n_doc,
        in_specs=[pl.BlockSpec(memory_space=pltpu.SMEM), anywhere, anywhere, vmem, vmem, vmem, anywhere, vmem, vmem, vmem],
        out_specs=[vmem] * n_doc,
        scratch_shapes=[
            pltpu.VMEM((n_pass, length, width), jnp.bfloat16),
            pltpu.VMEM((width, width), jnp.bfloat16),
            pltpu.VMEM((width, terms), jnp.bfloat16),
            pltpu.VMEM((rows, width), jnp.bfloat16),
            pltpu.VMEM((chunk, width), jnp.float32),
            pltpu.VMEM((n_pass + 1, 8, terms), jnp.float32),
            pltpu.VMEM((8, terms), jnp.float32),
            pltpu.VMEM((n_pass, n_hi, lo_terms), jnp.float32),
            pltpu.VMEM((2 * n_pass * n_hi, lo_terms), jnp.bfloat16),
            pltpu.VMEM((n_slot, 1, n_query), jnp.int32),
            pltpu.SMEM((8,), jnp.int32),
            pltpu.SemaphoreType.DMA((n_pass,)),
            pltpu.SemaphoreType.DMA,
            pltpu.SemaphoreType.DMA((terms // tile,)),
        ],
        compiler_params=pltpu.CompilerParams(vmem_limit_bytes=50 * 2**20),
    )(
        lengths,
        hidden,
        w_trans,
        b_trans[None],
        ln_gain[None],
        ln_bias[None],
        w_decode,
        b_decode[None],
        query_ids.T,
        query_wts.T,
    )
    ratio = max(n_doc // n_voc, 1)
    voc = lax.axis_index("voc")
    doc = lax.axis_index("doc")
    out = jnp.zeros((ratio, n_pass, q_own), jnp.float32)
    for r in range(n_doc):
        pairs = [
            (d * n_voc + v, ((d % ratio) * n_voc + v + r) % n_doc * n_voc + d // ratio)
            for d in range(n_doc)
            for v in range(n_voc)
        ]
        got = lax.ppermute(blocks[r], ("doc", "voc"), pairs)
        if ratio == 1:
            out = got[None] if r == 0 else out + got[None]
        else:
            place = lax.rem(doc - r + n_doc, n_doc) // n_voc
            mine = jnp.arange(ratio)[:, None, None] == place
            out = out + jnp.where(mine, got[None], 0.0)
    return out.reshape(ratio * n_pass, q_own)


def solution(mesh):
    return jax.shard_map(
        functools.partial(shards, mesh.shape["doc"], mesh.shape["voc"]),
        mesh=mesh,
        in_specs=(
            P(("grp", "doc"), None, None),
            P(("grp", "doc")),
            P(),
            P(),
            P(),
            P(),
            P(None, "voc"),
            P("voc"),
            P("grp", None),
            P("grp", None),
        ),
        out_specs=P(("grp", "voc"), "doc"),
        check_vma=False,
    )
```

```python
import functools

import jax
import jax.numpy as jnp
from jax import lax
from jax.experimental import pallas as pl
from jax.experimental.pallas import tpu as pltpu
from jax.sharding import PartitionSpec as P

eps = 1e-06
score_scale = 1.0 / 1024.0
group_rows = 16
lo_terms = 256
unroll = 2
half_root = 0.7071067811865476


def ceil_to(value, unit):
    return -(-value // unit) * unit


def largest_tile(width, unit, limit):
    best = unit
    for size in range(unit, min(width, limit) + 1, unit):
        if width % size == 0:
            best = size
    return best


def norm_rows(pre, bias, gain, shift):
    x = pre + bias
    active = x * (1.0 + lax.erf(x * half_root))
    width = active.shape[-1]
    centre = active - jnp.sum(active, -1, keepdims=True) * (1.0 / width)
    spread = jnp.sum(centre * centre, -1, keepdims=True) * (1.0 / width)
    return centre * lax.rsqrt(spread + 4.0 * eps) * gain + shift


def compact(ids, wts, start, width, slots_ref):
    local = ids - start
    inside = (local >= 0) & (local < width)
    count = local.shape[0]
    outside = jnp.where(inside, 0, 1)

    def up(x, s):
        return jnp.concatenate([x[s:], jnp.zeros_like(x[:s])], 0)

    def down(x, s):
        return jnp.concatenate([jnp.zeros_like(x[:s]), x[:-s]], 0)

    before = outside
    step = 1
    while step < count:
        before = before + down(before, step)
        step *= 2
    key = jnp.where(inside, (before << 23) | (local << 8) | wts, 0)
    step, bit = 1, 23
    while step < count:
        moves = (key >> bit) & 1
        stay = jnp.where(moves == 0, key, 0)
        come = jnp.where(moves == 0, 0, key)
        key = stay | up(come, step)
        step *= 2
        bit += 1
    key = key & ((1 << 23) - 1)
    for k in range(count):
        slots_ref[k] = key[k : k + 1]
    return count - before[count - 1 :]


def kernel(
    sizes,
    len_ref,
    hid_hbm,
    wt_hbm,
    bt_hbm,
    gain_hbm,
    shift_hbm,
    wd_hbm,
    bd_hbm,
    ids_hbm,
    wts_hbm,
    *rest,
):
    n_pass, length, width, terms, n_doc, n_voc, q_own, chunk, tile = sizes
    outs = rest[:n_doc]
    (hid, wt, bt, gain, shift, wd, bd, ids, wts, tok, cur, stage, pre, acc, carry, tabf, tab, slots, part,
     sem_h, sem_s, sem_w) = rest[n_doc:]
    n_tile = terms // tile
    n_group = chunk // group_rows
    n_hi = tabf.shape[1]
    n_query = n_doc * q_own

    hid_copies = [pltpu.make_async_copy(hid_hbm.at[p], hid.at[p], sem_h.at[p]) for p in range(n_pass)]
    wd_copies = [
        pltpu.make_async_copy(
            wd_hbm.at[:, pl.ds(t * tile, tile)], wd.at[:, pl.ds(t * tile, tile)], sem_w.at[t]
        )
        for t in range(n_tile)
    ]
    small = [(ids_hbm, ids), (wts_hbm, wts), (wt_hbm, wt), (bt_hbm, bt), (gain_hbm, gain), (shift_hbm, shift), (bd_hbm, bd)]
    small_copies = [pltpu.make_async_copy(a, b, sem_s.at[i]) for i, (a, b) in enumerate(small)]
    for copy in small_copies[:2] + hid_copies[:2] + small_copies[2:6] + hid_copies[2:] + wd_copies + small_copies[6:]:
        copy.start()

    doc, voc = lax.axis_index("doc"), lax.axis_index("voc")
    small_copies[0].wait()
    small_copies[1].wait()
    lane_counts = compact(ids[...], wts[...], voc * terms, terms, slots)
    most = jnp.max(lane_counts)

    at = jnp.int32(0)
    starts = []
    for p in range(n_pass):
        starts.append(at)
        at = at + (len_ref[p] + (group_rows - 1)) // group_rows
    starts.append(at)
    n_chunk = (at + (n_group - 1)) // n_group

    for p in range(n_pass):
        hid_copies[p].wait()
        base = pl.multiple_of(starts[p] * group_rows, group_rows)
        tok[pl.ds(base, length), :] = hid[p]
        last = (len_ref[p] - 1) // group_rows * group_rows
        rows = hid[p, pl.ds(pl.multiple_of(last, group_rows), group_rows), :].astype(jnp.float32)
        live = lax.broadcasted_iota(jnp.int32, rows.shape, 0) < len_ref[p] - last
        fixed = jnp.where(live, rows, rows[0:1])
        tok[pl.ds(pl.multiple_of(base + last, group_rows), group_rows), :] = fixed.astype(jnp.bfloat16)
    for copy in small_copies[2:6]:
        copy.wait()
    bias_row, gain_row, shift_row = (ref[...].reshape(1, width) for ref in (bt, gain, shift))

    def project(c):
        rows = pl.ds(pl.multiple_of(c * chunk, group_rows), chunk)
        pre[...] = jnp.dot(tok[rows, :], wt[...], preferred_element_type=jnp.float32)

    def normalise(g, to):
        rows = slice(g * group_rows, (g + 1) * group_rows)
        to[rows, :] = norm_rows(pre[rows, :], bias_row, gain_row, shift_row).astype(jnp.bfloat16)

    project(0)
    for g in range(n_group):
        normalise(g, cur)
    carry[...] = jnp.zeros_like(carry)

    def decode(c, ahead, arrive):
        segs, firsts = [], []
        for g in range(n_group):
            group = c * n_group + g
            seg = jnp.int32(0)
            first = group == 0
            for p in range(1, n_pass + 1):
                seg = seg + jnp.where(group >= starts[p], 1, 0)
                first = first | (group == starts[p])
            segs.append(seg)
            firsts.append(first)
        if ahead:
            project(c + 1)
        for t in range(n_tile):
            if arrive:
                wd_copies[t].wait()
            cols = slice(t * tile, (t + 1) * tile)
            logits = jnp.dot(cur[...], wd[:, cols], preferred_element_type=jnp.float32)
            run = carry[:, cols]
            for g in range(n_group):
                r = g * group_rows
                top = jnp.maximum(logits[r : r + 8], logits[r + 8 : r + 16])
                run = jnp.where(firsts[g], top, jnp.maximum(run, top))
                acc[segs[g], :, cols] = run
            carry[:, cols] = run
            if ahead:
                for g in range(n_group * t // n_tile, n_group * (t + 1) // n_tile):
                    normalise(g, stage)
        if ahead:
            cur[...] = stage[...]

    decode(0, True, True)

    @pl.loop(1, n_chunk)
    def _(c):
        decode(c, True, False)

    small_copies[6].wait()
    tabf[...] = jnp.zeros_like(tabf)
    for h in range(-(-terms // lo_terms)):
        cols = slice(h * lo_terms, min((h + 1) * lo_terms, terms))
        size = cols.stop - cols.start
        bias = bd[cols].reshape(1, size)
        for p in range(n_pass):
            tabf[p, h : h + 1, :size] = jnp.max(acc[p, :, cols], 0, keepdims=True) + bias
    for p in range(n_pass):
        impacts = jnp.log1p(jnp.maximum(tabf[p], 0.0))
        upper = impacts.astype(jnp.bfloat16)
        lower = (impacts - upper.astype(jnp.float32)).astype(jnp.bfloat16)
        tab[p * n_hi : (p + 1) * n_hi, :] = upper
        tab[(n_pass + p) * n_hi : (n_pass + p + 1) * n_hi, :] = lower

    sub = lax.broadcasted_iota(jnp.int32, (lo_terms, q_own), 0)
    hi_sub = lax.broadcasted_iota(jnp.int32, (n_hi, q_own), 0)
    part[...] = jnp.zeros_like(part)

    @pl.loop(0, (most + unroll - 1) // unroll)
    def _(step):
        for block in range(n_doc):
            lanes = slice(block * q_own, (block + 1) * q_own)
            sums = [part[p, :, lanes] for p in range(n_pass)]
            for u in range(unroll):
                key = slots[step * unroll + u, :, lanes]
                weight = (key & 255).astype(jnp.float32)
                term = key >> 8
                hot = jnp.where(sub == (term & (lo_terms - 1)), 1.0, 0.0).astype(jnp.bfloat16)
                found = jnp.dot(tab[...], hot, preferred_element_type=jnp.float32)
                pick = jnp.where(hi_sub == term // lo_terms, weight, 0.0)
                for p in range(n_pass):
                    a = p * n_hi
                    b = (n_pass + p) * n_hi
                    value = (found[a : a + n_hi] + found[b : b + n_hi]) * pick
                    sums[p] = sums[p] + jnp.sum(value.reshape(n_hi // 8, 8, q_own), 0)
            for p in range(n_pass):
                part[p, :, lanes] = sums[p]

    ratio = max(n_doc // n_voc, 1)
    for r in range(n_doc):
        block = lax.rem(lax.rem(doc, ratio) * n_voc + voc + r, n_doc)
        lanes = pl.ds(pl.multiple_of(block * q_own, 128), q_own)
        for p in range(n_pass):
            outs[r][p : p + 1, :] = jnp.sum(part[p, :, lanes], 0, keepdims=True) * score_scale


def shards(
    n_doc, n_voc, hidden, lengths, w_trans, b_trans, ln_gain, ln_bias, w_decode, b_decode, query_ids, query_wts
):
    n_pass, length, width = hidden.shape
    terms = w_decode.shape[1]
    n_query, n_slot = query_ids.shape
    q_own = n_query // n_doc
    chunk = 256
    tile = largest_tile(terms, 128, 3840)
    n_hi = ceil_to(-(-terms // lo_terms), 8)
    rows = ceil_to(n_pass * length, chunk) + chunk
    sizes = (n_pass, length, width, terms, n_doc, n_voc, q_own, chunk, tile)
    vmem = pl.BlockSpec(memory_space=pltpu.VMEM)
    anywhere = pl.BlockSpec(memory_space=pl.ANY)
    blocks = pl.pallas_call(
        functools.partial(kernel, sizes),
        out_shape=[jax.ShapeDtypeStruct((n_pass, q_own), jnp.float32)] * n_doc,
        in_specs=[pl.BlockSpec(memory_space=pltpu.SMEM)] + [anywhere] * 9,
        out_specs=[vmem] * n_doc,
        scratch_shapes=[
            pltpu.VMEM((n_pass, length, width), jnp.bfloat16),
            pltpu.VMEM((width, width), jnp.bfloat16),
            pltpu.VMEM((width,), jnp.float32),
            pltpu.VMEM((width,), jnp.float32),
            pltpu.VMEM((width,), jnp.float32),
            pltpu.VMEM((width, terms), jnp.bfloat16),
            pltpu.VMEM((terms,), jnp.float32),
            pltpu.VMEM((n_slot, n_query), jnp.int32),
            pltpu.VMEM((n_slot, n_query), jnp.int32),
            pltpu.VMEM((rows, width), jnp.bfloat16),
            pltpu.VMEM((chunk, width), jnp.bfloat16),
            pltpu.VMEM((chunk, width), jnp.bfloat16),
            pltpu.VMEM((chunk, width), jnp.float32),
            pltpu.VMEM((n_pass + 1, 8, terms), jnp.float32),
            pltpu.VMEM((8, terms), jnp.float32),
            pltpu.VMEM((n_pass, n_hi, lo_terms), jnp.float32),
            pltpu.VMEM((2 * n_pass * n_hi, lo_terms), jnp.bfloat16),
            pltpu.VMEM((n_slot, 1, n_query), jnp.int32),
            pltpu.VMEM((n_pass, 8, n_query), jnp.float32),
            pltpu.SemaphoreType.DMA((n_pass,)),
            pltpu.SemaphoreType.DMA((7,)),
            pltpu.SemaphoreType.DMA((terms // tile,)),
        ],
        compiler_params=pltpu.CompilerParams(vmem_limit_bytes=60 * 10**6),
    )(
        lengths,
        hidden,
        w_trans,
        b_trans,
        ln_gain,
        ln_bias,
        w_decode,
        b_decode,
        query_ids.T,
        query_wts.T,
    )
    ratio = max(n_doc // n_voc, 1)
    voc = lax.axis_index("voc")
    doc = lax.axis_index("doc")
    out = jnp.zeros((ratio, n_pass, q_own), jnp.float32)
    for r in range(n_doc):
        pairs = [
            (d * n_voc + v, ((d % ratio) * n_voc + v + r) % n_doc * n_voc + d // ratio)
            for d in range(n_doc)
            for v in range(n_voc)
        ]
        got = lax.ppermute(blocks[r], ("doc", "voc"), pairs)
        if ratio == 1:
            out = got[None] if r == 0 else out + got[None]
        else:
            place = lax.rem(doc - r + n_doc, n_doc) // n_voc
            mine = jnp.arange(ratio)[:, None, None] == place
            out = out + jnp.where(mine, got[None], 0.0)
    return out.reshape(ratio * n_pass, q_own)


def solution(mesh):
    return jax.shard_map(
        functools.partial(shards, mesh.shape["doc"], mesh.shape["voc"]),
        mesh=mesh,
        in_specs=(
            P(("grp", "doc"), None, None),
            P(("grp", "doc")),
            P(),
            P(),
            P(),
            P(),
            P(None, "voc"),
            P("voc"),
            P("grp", None),
            P("grp", None),
        ),
        out_specs=P(("grp", "voc"), "doc"),
        check_vma=False,
    )
```

```python
import functools

import jax
import jax.numpy as jnp
from jax import lax
from jax.experimental import pallas as pl
from jax.experimental.pallas import tpu as pltpu
from jax.sharding import PartitionSpec as P

eps = 1e-06
score_scale = 1.0 / 1024.0
group_rows = 16
lo_terms = 256
unroll = 4
half_root = 0.7071067811865476


def ceil_to(value, unit):
    return -(-value // unit) * unit


def largest_tile(width, unit, limit):
    best = unit
    for size in range(unit, min(width, limit) + 1, unit):
        if width % size == 0:
            best = size
    return best


def norm_rows(pre, bias, gain, shift):
    x = pre + bias
    active = x * (1.0 + lax.erf(x * half_root))
    width = active.shape[-1]
    centre = active - jnp.sum(active, -1, keepdims=True) * (1.0 / width)
    spread = jnp.sum(centre * centre, -1, keepdims=True) * (1.0 / width)
    return centre * lax.rsqrt(spread + 4.0 * eps) * gain + shift


def meet(place, r, n_doc):
    return (place + (2 * r + 1)) % n_doc


def compact(ids, wts, start, width, slots_ref):
    local = ids - start
    inside = (local >= 0) & (local < width)
    count = local.shape[0]
    outside = jnp.where(inside, 0, 1)

    def up(x, s):
        return jnp.concatenate([x[s:], jnp.zeros_like(x[:s])], 0)

    def down(x, s):
        return jnp.concatenate([jnp.zeros_like(x[:s]), x[:-s]], 0)

    before = outside
    step = 1
    while step < count:
        before = before + down(before, step)
        step *= 2
    key = jnp.where(inside, (before << 23) | (local << 8) | wts, 0)
    step, bit = 1, 23
    while step < count:
        moves = (key >> bit) & 1
        stay = jnp.where(moves == 0, key, 0)
        come = jnp.where(moves == 0, 0, key)
        key = stay | up(come, step)
        step *= 2
        bit += 1
    key = key & ((1 << 23) - 1)
    for k in range(count):
        slots_ref[k] = key[k : k + 1]
    return count - before[count - 1 :]


def kernel(
    sizes,
    len_ref,
    hid_hbm,
    wt_hbm,
    bt_hbm,
    gain_hbm,
    shift_hbm,
    wd_hbm,
    bd_hbm,
    ids_hbm,
    wts_hbm,
    *rest,
):
    n_pass, length, width, terms, n_doc, n_voc, q_own, chunk, tile, part_tile = sizes
    wd_parts = range(terms // part_tile)
    n_round = n_doc // 2
    outs = rest[:n_round]
    (hid, wt, bt, gain, shift, wd, bd, ids, wts, tok, cur, stage, pre, acc, carry, tabf, tab, slots, part, lane_counts,
     sem_h, sem_s, sem_w) = rest[n_round:]
    n_group = chunk // group_rows
    tails = (8, 12, n_group)
    n_hi = tabf.shape[1]
    n_query = n_doc * q_own

    hid_copies = [pltpu.make_async_copy(hid_hbm.at[p], hid.at[p], sem_h.at[p]) for p in range(n_pass)]
    wd_copies = [
        pltpu.make_async_copy(
            wd_hbm.at[:, pl.ds(t * part_tile, part_tile)],
            wd.at[:, pl.ds(t * part_tile, part_tile)],
            sem_w.at[t],
        )
        for t in wd_parts
    ]
    small = [(ids_hbm, ids), (wts_hbm, wts), (wt_hbm, wt), (bt_hbm, bt), (gain_hbm, gain), (shift_hbm, shift), (bd_hbm, bd)]
    small_copies = [pltpu.make_async_copy(a, b, sem_s.at[i]) for i, (a, b) in enumerate(small)]
    for copy in small_copies[2:3] + hid_copies + small_copies[3:6] + wd_copies[:1] + small_copies[:2] + small_copies[6:]:
        copy.start()

    doc, voc = lax.axis_index("doc"), lax.axis_index("voc")

    at = jnp.int32(0)
    starts = []
    for p in range(n_pass):
        starts.append(at)
        at = at + (len_ref[p] + (group_rows - 1)) // group_rows
    starts.append(at)
    total = at

    for p in range(n_pass):
        hid_copies[p].wait()
        if p == n_pass // 2:
            for copy in wd_copies[1:2]:
                copy.start()
        base = pl.multiple_of(starts[p] * group_rows, group_rows)
        tok[pl.ds(base, length), :] = hid[p]
        last = (len_ref[p] - 1) // group_rows * group_rows
        rows = hid[p, pl.ds(pl.multiple_of(last, group_rows), group_rows), :].astype(jnp.float32)
        live = lax.broadcasted_iota(jnp.int32, rows.shape, 0) < len_ref[p] - last
        fixed = jnp.where(live, rows, rows[0:1])
        tok[pl.ds(pl.multiple_of(base + last, group_rows), group_rows), :] = fixed.astype(jnp.bfloat16)
    for copy in wd_copies[2:3]:
        copy.start()
    for copy in small_copies[2:6]:
        copy.wait()
    bias_row, gain_row, shift_row = (ref[...].reshape(1, width) for ref in (bt, gain, shift))

    def project(c):
        rows = pl.ds(pl.multiple_of(c * chunk, group_rows), chunk)
        pre[...] = jnp.dot(tok[rows, :], wt[...], preferred_element_type=jnp.float32)

    def normalise(g, to):
        rows = slice(g * group_rows, (g + 1) * group_rows)
        to[rows, :] = norm_rows(pre[rows, :], bias_row, gain_row, shift_row).astype(jnp.bfloat16)

    project(0)
    for g in range(n_group):
        normalise(g, cur)
    small_copies[0].wait()
    small_copies[1].wait()
    carry[...] = jnp.zeros_like(carry)

    def decode(c, groups, ahead, arrive):
        segs, firsts = [], []
        for g in range(groups):
            group = c * n_group + g
            seg = jnp.int32(0)
            first = group == 0
            for p in range(1, n_pass + 1):
                seg = seg + jnp.where(group >= starts[p], 1, 0)
                first = first | (group == starts[p])
            segs.append(seg)
            firsts.append(first)
        size = part_tile if arrive else tile
        n_tile = terms // size
        if ahead:
            project(c + 1)
        for t in range(n_tile):
            if arrive:
                for copy in wd_copies[t + 3 : t + 4]:
                    copy.start()
                wd_copies[t].wait()
            cols = slice(t * size, (t + 1) * size)
            logits = jnp.dot(
                cur[: groups * group_rows, :], wd[:, cols], preferred_element_type=jnp.float32
            )
            run = carry[:, cols]
            for g in range(groups):
                r = g * group_rows
                top = jnp.maximum(logits[r : r + 8], logits[r + 8 : r + 16])
                run = jnp.where(firsts[g], top, jnp.maximum(run, top))
                acc[segs[g], :, cols] = run
            carry[:, cols] = run
            if ahead:
                for g in range(n_group * t // n_tile, n_group * (t + 1) // n_tile):
                    normalise(g, stage)
            if arrive and t == 0:
                lane_counts[...] = compact(ids[...], wts[...], voc * terms, terms, slots)
        if ahead:
            cur[...] = stage[...]

    decode(0, n_group, True, True)
    n_full = jnp.maximum(total // n_group, 1)

    @pl.loop(1, n_full)
    def _(c):
        decode(c, n_group, True, False)

    left = total - n_full * n_group
    for low, high in zip((0,) + tails[:-1], tails):

        @pl.when((left > low) & (left <= high))
        def _(high=high):
            decode(n_full, high, False, False)

    most = jnp.max(lane_counts[...])

    small_copies[6].wait()
    tabf[...] = jnp.zeros_like(tabf)
    for h in range(-(-terms // lo_terms)):
        cols = slice(h * lo_terms, min((h + 1) * lo_terms, terms))
        size = cols.stop - cols.start
        bias = bd[cols].reshape(1, size)
        for p in range(n_pass):
            tabf[p, h : h + 1, :size] = jnp.max(acc[p, :, cols], 0, keepdims=True) + bias
    for p in range(n_pass):
        impacts = jnp.log1p(jnp.maximum(tabf[p], 0.0))
        upper = impacts.astype(jnp.bfloat16)
        lower = (impacts - upper.astype(jnp.float32)).astype(jnp.bfloat16)
        tab[p * n_hi : (p + 1) * n_hi, :] = upper
        tab[(n_pass + p) * n_hi : (n_pass + p + 1) * n_hi, :] = lower

    sub = lax.broadcasted_iota(jnp.int32, (lo_terms, q_own), 0)
    hi_sub = lax.broadcasted_iota(jnp.int32, (n_hi, q_own), 0)
    part[...] = jnp.zeros_like(part)

    def add_slots(first, count):
        for block in range(n_doc):
            lanes = slice(block * q_own, (block + 1) * q_own)
            sums = [part[p, :, lanes] for p in range(n_pass)]
            for u in range(count):
                key = slots[first + u, :, lanes]
                weight = (key & 255).astype(jnp.float32)
                term = key >> 8
                hot = jnp.where(sub == (term & (lo_terms - 1)), 1.0, 0.0).astype(jnp.bfloat16)
                found = jnp.dot(tab[...], hot, preferred_element_type=jnp.float32)
                pick = jnp.where(hi_sub == term // lo_terms, weight, 0.0)
                for p in range(n_pass):
                    a = p * n_hi
                    b = (n_pass + p) * n_hi
                    value = (found[a : a + n_hi] + found[b : b + n_hi]) * pick
                    sums[p] = sums[p] + jnp.sum(value.reshape(n_hi // 8, 8, q_own), 0)
            for p in range(n_pass):
                part[p, :, lanes] = sums[p]

    n_many = most // unroll

    @pl.loop(0, n_many)
    def _(step):
        add_slots(step * unroll, unroll)

    @pl.loop(n_many * unroll, most)
    def _(k):
        add_slots(k, 1)

    ratio = max(n_doc // n_voc, 1)
    for r in range(n_round):
        target = meet(lax.rem(doc, ratio) * n_voc + voc, r, n_doc)
        for side in range(2):
            block = target + side - 2 * side * lax.rem(target, 2)
            lanes = pl.ds(pl.multiple_of(block * q_own, 128), q_own)
            for p in range(n_pass):
                outs[r][p : p + 1, side * q_own : (side + 1) * q_own] = (
                    jnp.sum(part[p, :, lanes], 0, keepdims=True) * score_scale
                )


def shards(
    n_doc, n_voc, hidden, lengths, w_trans, b_trans, ln_gain, ln_bias, w_decode, b_decode, query_ids, query_wts
):
    n_pass, length, width = hidden.shape
    terms = w_decode.shape[1]
    n_query, n_slot = query_ids.shape
    q_own = n_query // n_doc
    chunk = 256
    tile = largest_tile(terms, 128, 7680)
    part_tile = largest_tile(terms, 128, 1280)
    n_hi = ceil_to(-(-terms // lo_terms), 8)
    rows = ceil_to(n_pass * length, chunk) + chunk
    sizes = (n_pass, length, width, terms, n_doc, n_voc, q_own, chunk, tile, part_tile)
    vmem = pl.BlockSpec(memory_space=pltpu.VMEM)
    anywhere = pl.BlockSpec(memory_space=pl.ANY)
    blocks = pl.pallas_call(
        functools.partial(kernel, sizes),
        out_shape=[jax.ShapeDtypeStruct((n_pass, 2 * q_own), jnp.float32)] * (n_doc // 2),
        in_specs=[pl.BlockSpec(memory_space=pltpu.SMEM)] + [anywhere] * 9,
        out_specs=[vmem] * (n_doc // 2),
        scratch_shapes=[
            pltpu.VMEM((n_pass, length, width), jnp.bfloat16),
            pltpu.VMEM((width, width), jnp.bfloat16),
            pltpu.VMEM((width,), jnp.float32),
            pltpu.VMEM((width,), jnp.float32),
            pltpu.VMEM((width,), jnp.float32),
            pltpu.VMEM((width, terms), jnp.bfloat16),
            pltpu.VMEM((terms,), jnp.float32),
            pltpu.VMEM((n_slot, n_query), jnp.int32),
            pltpu.VMEM((n_slot, n_query), jnp.int32),
            pltpu.VMEM((rows, width), jnp.bfloat16),
            pltpu.VMEM((chunk, width), jnp.bfloat16),
            pltpu.VMEM((chunk, width), jnp.bfloat16),
            pltpu.VMEM((chunk, width), jnp.float32),
            pltpu.VMEM((n_pass + 1, 8, terms), jnp.float32),
            pltpu.VMEM((8, terms), jnp.float32),
            pltpu.VMEM((n_pass, n_hi, lo_terms), jnp.float32),
            pltpu.VMEM((2 * n_pass * n_hi, lo_terms), jnp.bfloat16),
            pltpu.VMEM((n_slot, 1, n_query), jnp.int32),
            pltpu.VMEM((n_pass, 8, n_query), jnp.float32),
            pltpu.VMEM((1, n_query), jnp.int32),
            pltpu.SemaphoreType.DMA((n_pass,)),
            pltpu.SemaphoreType.DMA((7,)),
            pltpu.SemaphoreType.DMA((terms // part_tile,)),
        ],
        compiler_params=pltpu.CompilerParams(vmem_limit_bytes=60 * 10**6),
    )(
        lengths,
        hidden,
        w_trans,
        b_trans,
        ln_gain,
        ln_bias,
        w_decode,
        b_decode,
        query_ids.T,
        query_wts.T,
    )
    ratio = max(n_doc // n_voc, 1)
    doc = lax.axis_index("doc")
    sums = None
    for r in range(n_doc // 2):
        pairs = [
            (d * n_voc + v, meet((d % ratio) * n_voc + v, r, n_doc) * n_voc + d // ratio)
            for d in range(n_doc)
            for v in range(n_voc)
        ]
        got = lax.ppermute(blocks[r], ("doc", "voc"), pairs)[None]
        if ratio > 1:
            place = lax.rem(doc + (n_doc - 2 * r - 1), n_doc) // n_voc
            got = jnp.where(jnp.arange(ratio)[:, None, None] == place, got, 0.0)
        sums = got if sums is None else sums + got
    kept, passed = sums[..., :q_own], sums[..., q_own:]
    out = kept + lax.ppermute(passed, "doc", [(d, d ^ 1) for d in range(n_doc)])
    return out.reshape(ratio * n_pass, q_own)


def solution(mesh):
    return jax.shard_map(
        functools.partial(shards, mesh.shape["doc"], mesh.shape["voc"]),
        mesh=mesh,
        in_specs=(
            P(("grp", "doc"), None, None),
            P(("grp", "doc")),
            P(),
            P(),
            P(),
            P(),
            P(None, "voc"),
            P("voc"),
            P("grp", None),
            P("grp", None),
        ),
        out_specs=P(("grp", "voc"), "doc"),
        check_vma=False,
    )
```

```python
import functools

import jax
import jax.numpy as jnp
from jax import lax
from jax.experimental import pallas as pl
from jax.experimental.pallas import tpu as pltpu
from jax.sharding import PartitionSpec as P

eps = 1e-06
score_scale = 1.0 / 1024.0
group_rows = 16
lo_terms = 256
unroll = 4
half_root = 0.7071067811865476


def ceil_to(value, unit):
    return -(-value // unit) * unit


def largest_tile(width, unit, limit):
    best = unit
    for size in range(unit, min(width, limit) + 1, unit):
        if width % size == 0:
            best = size
    return best


def norm_rows(pre, bias, gain, shift):
    x = pre + bias
    active = x * (1.0 + lax.erf(x * half_root))
    width = active.shape[-1]
    centre = active - jnp.sum(active, -1, keepdims=True) * (1.0 / width)
    spread = jnp.sum(centre * centre, -1, keepdims=True) * (1.0 / width)
    return centre * lax.rsqrt(spread + 4.0 * eps) * gain + shift


def meet(place, r, n_doc):
    return (place + (2 * r + 1)) % n_doc


def compact(ids, wts, start, width, slots_ref):
    local = ids - start
    inside = (local >= 0) & (local < width)
    count = local.shape[0]
    outside = jnp.where(inside, 0, 1)

    def up(x, s):
        return jnp.concatenate([x[s:], jnp.zeros_like(x[:s])], 0)

    def down(x, s):
        return jnp.concatenate([jnp.zeros_like(x[:s]), x[:-s]], 0)

    before = outside
    step = 1
    while step < count:
        before = before + down(before, step)
        step *= 2
    key = jnp.where(inside, (before << 23) | (local << 8) | wts, 0)
    step, bit = 1, 23
    while step < count:
        moves = (key >> bit) & 1
        stay = jnp.where(moves == 0, key, 0)
        come = jnp.where(moves == 0, 0, key)
        key = stay | up(come, step)
        step *= 2
        bit += 1
    key = key & ((1 << 23) - 1)
    for k in range(count):
        slots_ref[k] = key[k : k + 1]
    return count - before[count - 1 :]


def kernel(
    sizes,
    len_ref,
    hid_hbm,
    wt_hbm,
    bt_hbm,
    gain_hbm,
    shift_hbm,
    wd_hbm,
    bd_hbm,
    ids_hbm,
    wts_hbm,
    *rest,
):
    n_pass, length, width, terms, n_doc, n_voc, q_own, chunk, tile, part_tile = sizes
    wd_parts = range(terms // part_tile)
    n_round = n_doc // 2
    outs = rest[:n_round]
    (hid, wt, bt, gain, shift, wd, bd, ids, wts, tok, cur, stage, pre, acc, carry, tabf, tab, slots, part, lane_counts,
     sem_h, sem_s, sem_w) = rest[n_round:]
    n_group = chunk // group_rows
    tails = (8, 12, n_group)
    n_hi = tabf.shape[1]
    n_query = n_doc * q_own

    hid_copies = [pltpu.make_async_copy(hid_hbm.at[p], hid.at[p], sem_h.at[p]) for p in range(n_pass)]
    wd_copies = [
        pltpu.make_async_copy(
            wd_hbm.at[:, pl.ds(t * part_tile, part_tile)],
            wd.at[:, pl.ds(t * part_tile, part_tile)],
            sem_w.at[t],
        )
        for t in wd_parts
    ]
    small = [(ids_hbm, ids), (wts_hbm, wts), (wt_hbm, wt), (bt_hbm, bt), (gain_hbm, gain), (shift_hbm, shift), (bd_hbm, bd)]
    small_copies = [pltpu.make_async_copy(a, b, sem_s.at[i]) for i, (a, b) in enumerate(small)]
    for copy in small_copies[2:3] + hid_copies + small_copies[3:6] + wd_copies[:1] + small_copies[:2] + small_copies[6:]:
        copy.start()

    doc, voc = lax.axis_index("doc"), lax.axis_index("voc")

    at = jnp.int32(0)
    starts = []
    for p in range(n_pass):
        starts.append(at)
        at = at + (len_ref[p] + (group_rows - 1)) // group_rows
    starts.append(at)
    total = at

    for p in range(n_pass):
        hid_copies[p].wait()
        if p == n_pass // 2:
            for copy in wd_copies[1:2]:
                copy.start()
        base = pl.multiple_of(starts[p] * group_rows, group_rows)
        tok[pl.ds(base, length), :] = hid[p]
        last = (len_ref[p] - 1) // group_rows * group_rows
        rows = hid[p, pl.ds(pl.multiple_of(last, group_rows), group_rows), :].astype(jnp.float32)
        live = lax.broadcasted_iota(jnp.int32, rows.shape, 0) < len_ref[p] - last
        fixed = jnp.where(live, rows, rows[0:1])
        tok[pl.ds(pl.multiple_of(base + last, group_rows), group_rows), :] = fixed.astype(jnp.bfloat16)
    for copy in wd_copies[2:3]:
        copy.start()
    for copy in small_copies[2:6]:
        copy.wait()
    bias_row, gain_row, shift_row = (ref[...].reshape(1, width) for ref in (bt, gain, shift))

    def project(c):
        rows = pl.ds(pl.multiple_of(c * chunk, group_rows), chunk)
        pre[...] = jnp.dot(tok[rows, :], wt[...], preferred_element_type=jnp.float32)

    def normalise(g, to):
        rows = slice(g * group_rows, (g + 1) * group_rows)
        to[rows, :] = norm_rows(pre[rows, :], bias_row, gain_row, shift_row).astype(jnp.bfloat16)

    project(0)
    for g in range(n_group):
        normalise(g, cur)
    small_copies[0].wait()
    small_copies[1].wait()
    carry[...] = jnp.zeros_like(carry)

    def decode(c, groups, ahead, arrive):
        segs, firsts = [], []
        for g in range(groups):
            group = c * n_group + g
            seg = jnp.int32(0)
            first = group == 0
            for p in range(1, n_pass + 1):
                seg = seg + jnp.where(group >= starts[p], 1, 0)
                first = first | (group == starts[p])
            segs.append(seg)
            firsts.append(first)
        size = part_tile if arrive else tile
        n_tile = terms // size
        if ahead:
            project(c + 1)
        for t in range(n_tile):
            if arrive:
                for copy in wd_copies[t + 3 : t + 4]:
                    copy.start()
                wd_copies[t].wait()
            cols = slice(t * size, (t + 1) * size)
            logits = jnp.dot(
                cur[: groups * group_rows, :], wd[:, cols], preferred_element_type=jnp.float32
            )
            run = carry[:, cols]
            for g in range(groups):
                r = g * group_rows
                top = jnp.maximum(logits[r : r + 8], logits[r + 8 : r + 16])
                run = jnp.where(firsts[g], top, jnp.maximum(run, top))
                acc[segs[g], :, cols] = run
            carry[:, cols] = run
            if ahead:
                for g in range(n_group * t // n_tile, n_group * (t + 1) // n_tile):
                    normalise(g, stage)
            if arrive and t == 0:
                lane_counts[...] = compact(ids[...], wts[...], voc * terms, terms, slots)
        if ahead:
            cur[...] = stage[...]

    decode(0, n_group, True, True)
    n_full = jnp.maximum(total // n_group, 1)

    @pl.loop(1, n_full)
    def _(c):
        decode(c, n_group, True, False)

    left = total - n_full * n_group
    for low, high in zip((0,) + tails[:-1], tails):

        @pl.when((left > low) & (left <= high))
        def _(high=high):
            decode(n_full, high, False, False)

    most = jnp.max(lane_counts[...])

    small_copies[6].wait()
    tabf[...] = jnp.zeros_like(tabf)
    for h in range(-(-terms // lo_terms)):
        cols = slice(h * lo_terms, min((h + 1) * lo_terms, terms))
        size = cols.stop - cols.start
        bias = bd[cols].reshape(1, size)
        for p in range(n_pass):
            tabf[p, h : h + 1, :size] = jnp.max(acc[p, :, cols], 0, keepdims=True) + bias
    for p in range(n_pass):
        impacts = jnp.log1p(jnp.maximum(tabf[p], 0.0))
        upper = impacts.astype(jnp.bfloat16)
        lower = (impacts - upper.astype(jnp.float32)).astype(jnp.bfloat16)
        tab[p * n_hi : (p + 1) * n_hi, :] = upper
        tab[(n_pass + p) * n_hi : (n_pass + p + 1) * n_hi, :] = lower

    sub = lax.broadcasted_iota(jnp.int32, (lo_terms, q_own), 0)
    hi_sub = lax.broadcasted_iota(jnp.int32, (n_hi, q_own), 0)
    part[...] = jnp.zeros_like(part)

    def add_slots(first, count):
        for block in range(n_doc):
            lanes = slice(block * q_own, (block + 1) * q_own)
            sums = [part[p, :, lanes] for p in range(n_pass)]
            for u in range(count):
                key = slots[first + u, :, lanes]
                weight = (key & 255).astype(jnp.float32)
                term = key >> 8
                hot = jnp.where(sub == (term & (lo_terms - 1)), 1.0, 0.0).astype(jnp.bfloat16)
                found = jnp.dot(tab[...], hot, preferred_element_type=jnp.float32)
                pick = jnp.where(hi_sub == term // lo_terms, weight, 0.0)
                for p in range(n_pass):
                    a = p * n_hi
                    b = (n_pass + p) * n_hi
                    value = (found[a : a + n_hi] + found[b : b + n_hi]) * pick
                    sums[p] = sums[p] + jnp.sum(value.reshape(n_hi // 8, 8, q_own), 0)
            for p in range(n_pass):
                part[p, :, lanes] = sums[p]

    n_many = most // unroll

    @pl.loop(0, n_many)
    def _(step):
        add_slots(step * unroll, unroll)

    @pl.loop(n_many * unroll, most)
    def _(k):
        add_slots(k, 1)

    ratio = max(n_doc // n_voc, 1)
    for r in range(n_round):
        target = meet(lax.rem(doc, ratio) * n_voc + voc, r, n_doc)
        for side in range(2):
            block = target + side - 2 * side * lax.rem(target, 2)
            lanes = pl.ds(pl.multiple_of(block * q_own, 128), q_own)
            for p in range(n_pass):
                outs[r][p : p + 1, side * q_own : (side + 1) * q_own] = (
                    jnp.sum(part[p, :, lanes], 0, keepdims=True) * score_scale
                )


def shards(
    n_doc, n_voc, hidden, lengths, w_trans, b_trans, ln_gain, ln_bias, w_decode, b_decode, query_ids, query_wts
):
    n_pass, length, width = hidden.shape
    terms = w_decode.shape[1]
    n_query, n_slot = query_ids.shape
    q_own = n_query // n_doc
    chunk = 256
    tile = largest_tile(terms, 128, 7680)
    part_tile = largest_tile(terms, 128, 2560)
    n_hi = ceil_to(-(-terms // lo_terms), 8)
    rows = ceil_to(n_pass * length, chunk) + chunk
    sizes = (n_pass, length, width, terms, n_doc, n_voc, q_own, chunk, tile, part_tile)
    vmem = pl.BlockSpec(memory_space=pltpu.VMEM)
    anywhere = pl.BlockSpec(memory_space=pl.ANY)
    blocks = pl.pallas_call(
        functools.partial(kernel, sizes),
        out_shape=[jax.ShapeDtypeStruct((n_pass, 2 * q_own), jnp.float32)] * (n_doc // 2),
        in_specs=[pl.BlockSpec(memory_space=pltpu.SMEM)] + [anywhere] * 9,
        out_specs=[vmem] * (n_doc // 2),
        scratch_shapes=[
            pltpu.VMEM((n_pass, length, width), jnp.bfloat16),
            pltpu.VMEM((width, width), jnp.bfloat16),
            pltpu.VMEM((width,), jnp.float32),
            pltpu.VMEM((width,), jnp.float32),
            pltpu.VMEM((width,), jnp.float32),
            pltpu.VMEM((width, terms), jnp.bfloat16),
            pltpu.VMEM((terms,), jnp.float32),
            pltpu.VMEM((n_slot, n_query), jnp.int32),
            pltpu.VMEM((n_slot, n_query), jnp.int32),
            pltpu.VMEM((rows, width), jnp.bfloat16),
            pltpu.VMEM((chunk, width), jnp.bfloat16),
            pltpu.VMEM((chunk, width), jnp.bfloat16),
            pltpu.VMEM((chunk, width), jnp.float32),
            pltpu.VMEM((n_pass + 1, 8, terms), jnp.float32),
            pltpu.VMEM((8, terms), jnp.float32),
            pltpu.VMEM((n_pass, n_hi, lo_terms), jnp.float32),
            pltpu.VMEM((2 * n_pass * n_hi, lo_terms), jnp.bfloat16),
            pltpu.VMEM((n_slot, 1, n_query), jnp.int32),
            pltpu.VMEM((n_pass, 8, n_query), jnp.float32),
            pltpu.VMEM((1, n_query), jnp.int32),
            pltpu.SemaphoreType.DMA((n_pass,)),
            pltpu.SemaphoreType.DMA((7,)),
            pltpu.SemaphoreType.DMA((terms // part_tile,)),
        ],
        compiler_params=pltpu.CompilerParams(vmem_limit_bytes=60 * 10**6),
    )(
        lengths,
        hidden,
        w_trans,
        b_trans,
        ln_gain,
        ln_bias,
        w_decode,
        b_decode,
        query_ids.T,
        query_wts.T,
    )
    ratio = max(n_doc // n_voc, 1)
    doc = lax.axis_index("doc")
    sums = None
    for r in range(n_doc // 2):
        pairs = [
            (d * n_voc + v, meet((d % ratio) * n_voc + v, r, n_doc) * n_voc + d // ratio)
            for d in range(n_doc)
            for v in range(n_voc)
        ]
        got = lax.ppermute(blocks[r], ("doc", "voc"), pairs)[None]
        if ratio > 1:
            place = lax.rem(doc + (n_doc - 2 * r - 1), n_doc) // n_voc
            got = jnp.where(jnp.arange(ratio)[:, None, None] == place, got, 0.0)
        sums = got if sums is None else sums + got
    kept, passed = sums[..., :q_own], sums[..., q_own:]
    out = kept + lax.ppermute(passed, "doc", [(d, d ^ 1) for d in range(n_doc)])
    return out.reshape(ratio * n_pass, q_own)


def solution(mesh):
    return jax.shard_map(
        functools.partial(shards, mesh.shape["doc"], mesh.shape["voc"]),
        mesh=mesh,
        in_specs=(
            P(("grp", "doc"), None, None),
            P(("grp", "doc")),
            P(),
            P(),
            P(),
            P(),
            P(None, "voc"),
            P("voc"),
            P("grp", None),
            P("grp", None),
        ),
        out_specs=P(("grp", "voc"), "doc"),
        check_vma=False,
    )
```
